512 devices in a mesh: dp: 32 (over z, core), expert: 16 (over x, y).
Axes of the slice: x: 4, y: 4, z: 16, core: 2. Of those that a mesh axis runs over, the one named last changes fastest.
Arguments:
- cotangent: bfloat16 [196608, 1024], P(('dp', 'expert')), may hold values from -0.119628906 to 0.119628906
- route: int32 [196608, 1], P(('dp', 'expert')), may hold values from 0 to 15; in each aligned block of 384 rows (0 to 383, 384 to 767, ...) at most 72 rows name the same one
- hidden: bfloat16 [32, 16, 1152, 768], P('dp', 'expert'), may hold values from -6 to 6
- master: float32 [16, 768, 1024], P('expert', 'dp'), may hold values from -0.21875 to 0.21875
- moment_one: float32 [16, 768, 1024], P('expert', 'dp'), may hold values from -1.8 to 1.8
- moment_two: float32 [16, 768, 1024], P('expert', 'dp'), may hold values from 0.05 to 0.5
Outputs:
- master_next: float32 [16, 768, 1024], P('expert', 'dp')
- moment_one_next: float32 [16, 768, 1024], P('expert', 'dp')
- moment_two_next: float32 [16, 768, 1024], P('expert', 'dp')
- weights: bfloat16 [16, 768, 1024], P('expert')
The draws below stay inside these ranges and needn't reach their ends.
Inputs may be any that keep to these rules, and one draw needn't show every extreme that they name: `route`: among the tokens of one device no expert is named more than 72 times, and on some device one expert is named exactly 72 times.
All inputs are finite; a program needn't handle non-finite values.
Results may differ from the reference program's by a relative error of at most 0.001.
Values may be sent and summed in bfloat16 or wider, within the bound.
No kernel may reach another device: no remote copies, remote signals or barrier semaphores. Data moves between devices by JAX's collectives and lax.ppermute only.
A program may use at most 64 MiB of HBM per device.

```python
import math
import jax
import jax.numpy as jnp
import numpy as np
from jax import lax

D = 1024
FF = 768
TOK_DEV = 384
STEP = 10
EXPERTS = 16
CAP = 72
RECV = 1152
TOKENS = 196608
N_DP = 32
N_EXPERT = 16


def levels(stream_key, dims, shards, least, high):
    level, own = 1.0, jax.random.fold_in(stream_key, 6)
    for dim, shards_of in shards:
        draws = jnp.exp(jax.random.uniform(jax.random.fold_in(own, dim), (shards_of,), jnp.float32, least / len(shards), high / len(shards)))
        level = level * jnp.repeat(draws, dims[dim] // shards_of).reshape([-1 if axis == dim else 1 for axis in range(len(dims))])
    return level


def shared_out(rng, own, number, rows, count, top, limit, lean):
    ranking = jax.random.permutation(rng, count)
    heavy_load, ordinary = shares(count, rows * top, limit, lean, True), shares(count, rows * top, limit, lean, False)
    places = jnp.arange(count)

    def named(tallies, rotation):
        used = int((tallies > 0).sum())
        fixed = max(1, used // 4)
        moved = fixed + (places - fixed + rotation * (used - fixed)) % max(1, count - fixed)
        return jnp.zeros((count,), jnp.int32).at[ranking[jnp.where(places < fixed, places, moved)]].set(jnp.asarray(tallies, jnp.int32))

    tallies = jnp.where(number % 4 == 0, named(heavy_load, number // 4), named(ordinary, number - number // 4 - 1))
    mixed = jax.random.permutation(jax.random.fold_in(own, 3), count)
    source_of, receiver = mixed[0:count // 2 * 2:2], mixed[1:count // 2 * 2:2]
    room = jnp.minimum(tallies[source_of] - 1, limit - tallies[receiver]) // 2
    room = jnp.where((source_of == ranking[0]) | (receiver == ranking[0]) | (tallies[receiver] == 0), 0, jnp.maximum(room, 0))
    moved = jax.random.randint(jax.random.fold_in(own, 4), (count // 2,), 0, 1 << 20) % (room + 1)
    tallies = tallies.at[source_of].add(-moved).at[receiver].add(moved)
    items = jnp.searchsorted(jnp.cumsum(tallies), jnp.arange(rows * top), side="right").astype(jnp.int32)
    table = items.reshape(top, rows).T
    table = table[jax.random.permutation(jax.random.fold_in(own, 1), rows)]
    rotation = jax.random.randint(jax.random.fold_in(own, 2), (rows, 1), 0, top)
    return jnp.take_along_axis(table, (jnp.arange(top)[None, :] + rotation) % top, axis=1)


def shares(amount, total, limit, lean, full):
    portions = [(1 << 20) // math.isqrt(rank ** lean) + 1 for rank in range(1, amount + 1)]
    largest = limit if full else min(limit, max(-(-total // amount), total * portions[0] // sum(portions)))
    least = 1 if total - largest >= amount - 1 else 0
    given, spare = [largest] + [least] * (amount - 1), total - largest - least * (amount - 1)
    while spare > 0:
        candidates = [i for i in range(1, amount) if given[i] < largest] or [i for i in range(1, amount) if given[i] < limit]
        pool, budget = sum([portions[i] for i in candidates]), spare
        for i in candidates:
            more = min(limit - given[i], max(1, budget * portions[i] // pool), spare)
            given[i] = given[i] + more
            spare = spare - more
    return np.array(given)


def centred(stream_key, dims, width, most, shards=(), kind=jnp.bfloat16):
    result = width * jax.random.normal(stream_key, dims, jnp.float32)
    if shards:
        result = result * levels(stream_key, dims, shards, -0.22, 0.18)
    return jnp.clip(result, -most, most).astype(kind)


def setup_inputs(seed: int = 0) -> dict:
    seeds = jax.random.split(jax.random.key(seed), 7)
    cotangent = centred(seeds[0], (TOKENS, D), 0.02, 0.119628906, ((0, 512),))
    route_keys = jax.random.split(jax.random.fold_in(seeds[1], 1), TOKENS // TOK_DEV)
    route_turns = jax.random.permutation(jax.random.fold_in(seeds[1], 3), TOKENS // TOK_DEV)
    route = jax.vmap(lambda own, number: shared_out(jax.random.fold_in(seeds[1], 2), own, number, TOK_DEV, EXPERTS, 1, CAP, 1))(route_keys, route_turns).reshape((TOKENS, 1))
    hidden = centred(seeds[2], (N_DP, EXPERTS, RECV, FF), 1.0, 6.0, ((0, 32), (1, 16)))
    master = centred(seeds[3], (EXPERTS, FF, D), FF ** -0.5, 0.21875, ((0, 16), (1, 32)), jnp.float32)
    moment_one = centred(seeds[4], (EXPERTS, FF, D), 0.3, 1.8, ((0, 16), (1, 32)), jnp.float32)
    moment_two = jnp.clip(jnp.exp(math.log(0.5) - 2.3025851 * jax.random.uniform(seeds[5], (EXPERTS, FF, D), jnp.float32) ** levels(seeds[5], (EXPERTS, FF, D), ((0, 16), (1, 32)), -0.2, 0.2)), 0.05, 0.5)
    return {"cotangent": cotangent, "route": route, "hidden": hidden, "master": master, "moment_one": moment_one, "moment_two": moment_two}


def reference(cotangent, route, hidden, master, moment_one, moment_two):
    cot_blocks = cotangent.reshape(N_DP, N_EXPERT, TOK_DEV, D)
    route_blocks = route.reshape(N_DP, N_EXPERT, TOK_DEV)
    expert_ids = jnp.arange(EXPERTS, dtype=jnp.int32)

    def per_replica(total, inputs):
        cot_rep, route_rep, hidden_rep = inputs
        one_hot = (route_rep[..., None] == expert_ids[None, None, :]).astype(jnp.int32)
        rank = lax.optimization_barrier(jnp.sum((jnp.cumsum(one_hot, axis=1) - one_hot) * one_hot, axis=-1))
        row_pos = jnp.arange(N_EXPERT, dtype=jnp.int32)[:, None] * CAP + rank
        received = jnp.zeros((EXPERTS, RECV, D), jnp.bfloat16).at[route_rep, row_pos].set(cot_rep)
        term = jnp.einsum('erf,erd->efd', hidden_rep.astype(jnp.float32), received.astype(jnp.float32))
        return (total + term, None)
    start = jnp.zeros((EXPERTS, FF, D), jnp.float32)
    gradient, _ = lax.scan(per_replica, start, (cot_blocks, route_blocks, hidden))
    moment_one_next = 0.9 * moment_one + 0.1 * gradient
    moment_two_next = 0.95 * moment_two + 0.05 * gradient * gradient
    step_dir = moment_one_next / (1.0 - 0.9 ** STEP) / (jnp.sqrt(moment_two_next / (1.0 - 0.95 ** STEP)) + 1e-08)
    master_next = master - 0.01 * (step_dir + 0.1 * master)
    weights = master_next.astype(jnp.bfloat16)
    return (master_next, moment_one_next, moment_two_next, weights)
```

```python
import jax
import jax.numpy as jnp
from jax import lax
from jax.experimental import pallas as pl
from jax.experimental.pallas import tpu as pltpu
from jax.sharding import PartitionSpec as P

STEP = 10
FIXED = 65536.0
SMALL = 16.0
WEIGHT = 131072.0


def pack_kernel(capacity, route_ref, cot_ref, out_ref):
    tokens = cot_ref.shape[0]
    rows = out_ref.shape[0]
    block = 144
    col = route_ref[...]
    earlier = lax.broadcasted_iota(jnp.int32, (tokens, tokens), 0)
    token = lax.broadcasted_iota(jnp.int32, (tokens, tokens), 1)
    row = jnp.sum(jnp.where(earlier == token, col, 0), axis=0, keepdims=True)
    same = jnp.where((col == row) & (earlier < token), 1, 0)
    dest = row * capacity + jnp.sum(same, axis=0, keepdims=True)
    cot = cot_ref[...]
    for start in range(0, rows, block):
        slot = lax.broadcasted_iota(jnp.int32, (block, tokens), 0) + start
        pick = jnp.where(slot == dest, 1.0, 0.0).astype(jnp.bfloat16)
        out_ref[start : start + block, :] = jnp.dot(
            pick, cot, preferred_element_type=jnp.float32
        ).astype(jnp.bfloat16)


def pack(route, cotangent, num_experts, capacity):
    tokens, features = cotangent.shape
    rows = num_experts * capacity
    return pl.pallas_call(
        lambda *refs: pack_kernel(capacity, *refs),
        out_shape=jax.ShapeDtypeStruct((rows, features), jnp.bfloat16),
        in_specs=[pl.BlockSpec(memory_space=pltpu.VMEM)] * 2,
        out_specs=pl.BlockSpec(memory_space=pltpu.VMEM),
        compiler_params=pltpu.CompilerParams(vmem_limit_bytes=32 * 1024 * 1024),
        cost_estimate=pl.CostEstimate(
            flops=2 * rows * tokens * features, bytes_accessed=2 * (rows + tokens) * features, transcendentals=0
        ),
    )(route, cotangent)


def local(cotangent, route, hidden, master, moment_one, moment_two):
    num_experts = lax.axis_size("expert")
    n_dp = lax.axis_size("dp")
    recv_rows = hidden.shape[2]
    capacity = recv_rows // num_experts
    features = cotangent.shape[1]
    ff = hidden.shape[3]
    share = ff // n_dp
    pairs = n_dp // 4
    dp = lax.axis_index("dp")
    core = dp % 2
    pair = dp // 4

    ring = [[4 * p + r for p in range(pairs)] for r in range(4)]
    sides = [[4 * p + c, 4 * p + 2 + c] for p in range(pairs) for c in range(2)]
    quads = [[4 * p + r for r in range(4)] for p in range(pairs)]

    state = jnp.concatenate([master, moment_one, moment_two], axis=0)
    states = lax.all_gather(state, "dp", axis=0, tiled=False, axis_index_groups=ring)

    packed = pack(route, cotangent, num_experts, capacity).reshape(num_experts, capacity, features)
    received = lax.all_to_all(packed, "expert", split_axis=0, concat_axis=0, tiled=True).reshape(
        recv_rows, features
    )
    grad = lax.dot_general(
        hidden[0, 0], received, (((0,), (0,)), ((), ())), preferred_element_type=jnp.float32
    ).reshape(pairs, 2, 2, share, features)

    def of_core(which):
        return lax.dynamic_index_in_dim(grad, which, axis=2, keepdims=False)

    theirs = (of_core(1 - core) * SMALL).astype(jnp.float16)
    swap = [(d, d ^ 1) for d in range(n_dp)]
    other = lax.ppermute(theirs, "dp", swap)
    summed = of_core(core) * SMALL + other.astype(jnp.float32)
    halves = lax.all_to_all(
        summed.astype(jnp.float16).transpose(1, 0, 2, 3), "dp", 0, 0, tiled=True, axis_index_groups=sides
    )
    quarter = halves[0].astype(jnp.float32) + halves[1].astype(jnp.float32)
    fixed = jnp.round(quarter * (FIXED / SMALL)).astype(jnp.int32).astype(jnp.uint32)
    total = lax.psum(fixed, "dp", axis_index_groups=ring)
    gradient = total.astype(jnp.int32).astype(jnp.float32) * (1.0 / FIXED)

    m_all, one_all, two_all = states[:, 0], states[:, 1], states[:, 2]
    one_next = 0.9 * one_all + 0.1 * gradient
    two_next = 0.95 * two_all + 0.05 * gradient * gradient
    step_dir = one_next / (1.0 - 0.9**STEP) / (jnp.sqrt(two_next / (1.0 - 0.95**STEP)) + 1e-08)
    master_next = m_all - 0.01 * (step_dir + 0.1 * m_all)

    def own(x):
        return lax.dynamic_index_in_dim(x, pair, axis=0, keepdims=True)

    coded = (lax.reduce_precision(master_next, 8, 7) * WEIGHT).astype(jnp.float16)
    gathered = lax.all_gather(coded, "dp", axis=0, tiled=False, axis_index_groups=quads)
    weights = (gathered.astype(jnp.float32) * (1.0 / WEIGHT)).astype(jnp.bfloat16)
    weights = weights.transpose(1, 0, 2, 3).reshape(1, ff, features)
    return (own(master_next), own(one_next), own(two_next), weights)


def solution(mesh):
    return jax.shard_map(
        local,
        mesh=mesh,
        in_specs=(
            P(("dp", "expert"), None),
            P(("dp", "expert"), None),
            P("dp", "expert", None, None),
            P("expert", "dp", None),
            P("expert", "dp", None),
            P("expert", "dp", None),
        ),
        out_specs=(
            P("expert", "dp", None),
            P("expert", "dp", None),
            P("expert", "dp", None),
            P("expert", None, None),
        ),
        check_vma=False,
    )
```

```python
import jax
import jax.numpy as jnp
from jax import lax
from jax.experimental import pallas as pl
from jax.experimental.pallas import tpu as pltpu
from jax.sharding import PartitionSpec as P

STEP = 10
SMALL = 16.0
WEIGHT = 131072.0


def pack_kernel(capacity, route_hbm, cot_hbm, out_hbm, route, cot, rows, route_sem, cot_sem, out_sems):
    tokens = cot.shape[0]
    block = 2 * capacity
    fetch_route = pltpu.make_async_copy(route_hbm, route, route_sem)
    fetch_cot = pltpu.make_async_copy(cot_hbm, cot, cot_sem)
    fetch_route.start()
    fetch_cot.start()
    fetch_route.wait()
    row = route[...]
    later = lax.broadcasted_iota(jnp.int32, (tokens, tokens), 1)
    token = lax.broadcasted_iota(jnp.int32, (tokens, tokens), 0)
    col = jnp.sum(jnp.where(later == token, row, 0), axis=1, keepdims=True)
    same = jnp.where((col == row) & (token < later), 1, 0)
    dest = row * capacity + jnp.sum(same, axis=0, keepdims=True)
    fetch_cot.wait()
    copies = []
    for part in range(rows.shape[0] // block):
        where = pl.ds(part * block, block)
        slot = lax.broadcasted_iota(jnp.int32, (block, tokens), 0) + part * block
        pick = jnp.where(slot == dest, 1.0, 0.0).astype(jnp.bfloat16)
        rows[where, :] = jnp.dot(pick, cot[...], preferred_element_type=jnp.float32).astype(jnp.bfloat16)
        copies.append(pltpu.make_async_copy(rows.at[where, :], out_hbm.at[where, :], out_sems.at[part]))
        copies[-1].start()
    for copy in copies:
        copy.wait()


def pack(route, cotangent, num_experts, capacity):
    tokens, features = cotangent.shape
    rows = num_experts * capacity
    return pl.pallas_call(
        lambda *refs: pack_kernel(capacity, *refs),
        out_shape=jax.ShapeDtypeStruct((rows, features), jnp.bfloat16),
        in_specs=[pl.BlockSpec(memory_space=pltpu.HBM)] * 2,
        out_specs=pl.BlockSpec(memory_space=pltpu.HBM),
        scratch_shapes=[
            pltpu.VMEM((1, tokens), jnp.int32),
            pltpu.VMEM((tokens, features), jnp.bfloat16),
            pltpu.VMEM((rows, features), jnp.bfloat16),
            pltpu.SemaphoreType.DMA,
            pltpu.SemaphoreType.DMA,
            pltpu.SemaphoreType.DMA((num_experts // 2,)),
        ],
        compiler_params=pltpu.CompilerParams(vmem_limit_bytes=60 * 1024 * 1024),
        cost_estimate=pl.CostEstimate(
            flops=2 * rows * tokens * features, bytes_accessed=2 * (rows + tokens) * features, transcendentals=0
        ),
    )(route.reshape(1, tokens), cotangent)


def product_kernel(units_ref, tokens_ref, out_ref):
    out_ref[...] = jnp.dot(units_ref[...], tokens_ref[...], preferred_element_type=jnp.float32) * SMALL


def product(units, tokens):
    rows, depth = units.shape
    features = tokens.shape[1]
    width = 512
    return pl.pallas_call(
        product_kernel,
        grid=(features // width,),
        out_shape=jax.ShapeDtypeStruct((rows, features), jnp.float32),
        in_specs=[pl.BlockSpec((rows, depth), lambda i: (0, 0)), pl.BlockSpec((depth, width), lambda i: (0, i))],
        out_specs=pl.BlockSpec((rows, width), lambda i: (0, i)),
        compiler_params=pltpu.CompilerParams(vmem_limit_bytes=16 * 1024 * 1024),
        cost_estimate=pl.CostEstimate(
            flops=2 * rows * depth * features,
            bytes_accessed=2 * depth * (rows + features) + 4 * rows * features,
            transcendentals=0,
        ),
    )(units, tokens)


def local(cotangent, route, hidden, master, moment_one, moment_two):
    num_experts = lax.axis_size("expert")
    n_dp = lax.axis_size("dp")
    recv_rows = hidden.shape[2]
    capacity = recv_rows // num_experts
    features = cotangent.shape[1]
    ff = hidden.shape[3]
    share = ff // n_dp
    chips = n_dp // 2
    pairs = n_dp // 4
    core = lax.axis_index("dp") % 2

    ring = [[4 * p + r for p in range(pairs)] for r in range(4)]
    sides = [[4 * p + c, 4 * p + 2 + c] for p in range(pairs) for c in range(2)]

    packed = pack(route, cotangent, num_experts, capacity).reshape(num_experts, capacity, features)
    received = lax.all_to_all(packed, "expert", split_axis=0, concat_axis=0, tiled=True).reshape(
        recv_rows, features
    )

    units = hidden[0, 0].T.reshape(chips, 2, share, recv_rows)

    def of_core(which):
        return lax.dynamic_index_in_dim(units, which, axis=1, keepdims=False).reshape(chips * share, recv_rows)

    units_mine, units_theirs = lax.optimization_barrier((of_core(core), of_core(1 - core)))
    theirs = product(units_theirs, received)
    other = lax.ppermute(theirs.astype(jnp.float16), "dp", [(d, d ^ 1) for d in range(n_dp)])
    mine = product(units_mine, received)
    summed = (mine + other.astype(jnp.float32)).astype(jnp.float16)
    summed = summed.reshape(pairs, 2, share, features).transpose(1, 0, 2, 3)
    halves = lax.all_to_all(summed, "dp", 0, 0, tiled=True, axis_index_groups=sides)
    quarter = (halves[0].astype(jnp.float32) + halves[1].astype(jnp.float32)).astype(jnp.float16)
    eighths = lax.all_to_all(quarter, "dp", 0, 0, tiled=True, axis_index_groups=ring)
    gradient = jnp.sum(eighths.astype(jnp.float32), axis=0, keepdims=True) * (1.0 / SMALL)

    one_next = 0.9 * moment_one + 0.1 * gradient
    two_next = 0.95 * moment_two + 0.05 * gradient * gradient
    step_dir = one_next / (1.0 - 0.9**STEP) / (jnp.sqrt(two_next / (1.0 - 0.95**STEP)) + 1e-08)
    master_next = master - 0.01 * (step_dir + 0.1 * master)
    coded = (lax.reduce_precision(master_next, 8, 7) * WEIGHT).astype(jnp.float16)
    gathered = lax.all_gather(coded, "dp", axis=1, tiled=True)
    weights = (gathered.astype(jnp.float32) * (1.0 / WEIGHT)).astype(jnp.bfloat16)
    return (master_next, one_next, two_next, weights)


def solution(mesh):
    return jax.shard_map(
        local,
        mesh=mesh,
        in_specs=(
            P(("dp", "expert"), None),
            P(("dp", "expert"), None),
            P("dp", "expert", None, None),
            P("expert", "dp", None),
            P("expert", "dp", None),
            P("expert", "dp", None),
        ),
        out_specs=(
            P("expert", "dp", None),
            P("expert", "dp", None),
            P("expert", "dp", None),
            P("expert", None, None),
        ),
        check_vma=False,
    )
```

```python
import jax
import jax.numpy as jnp
from jax import lax
from jax.experimental import pallas as pl
from jax.experimental.pallas import tpu as pltpu
from jax.sharding import PartitionSpec as P

STEP = 10
SMALL = 16.0
WEIGHT = 131072.0


def pack_kernel(capacity, route_ref, cot_ref, out_ref):
    tokens = cot_ref.shape[0]
    block = 2 * capacity
    row = route_ref[...]
    later = lax.broadcasted_iota(jnp.int32, (tokens, tokens), 1)
    token = lax.broadcasted_iota(jnp.int32, (tokens, tokens), 0)
    col = jnp.sum(jnp.where(later == token, row, 0), axis=1, keepdims=True)
    same = jnp.where((col == row) & (token < later), 1, 0)
    dest = row * capacity + jnp.sum(same, axis=0, keepdims=True)
    for start in range(0, out_ref.shape[0], block):
        slot = lax.broadcasted_iota(jnp.int32, (block, tokens), 0) + start
        pick = jnp.where(slot == dest, 1.0, 0.0).astype(jnp.bfloat16)
        out_ref[start : start + block, :] = jnp.dot(
            pick, cot_ref[...], preferred_element_type=jnp.float32
        ).astype(jnp.bfloat16)


def pack(route, cotangent, num_experts, capacity):
    tokens, features = cotangent.shape
    rows = num_experts * capacity
    return pl.pallas_call(
        lambda *refs: pack_kernel(capacity, *refs),
        out_shape=jax.ShapeDtypeStruct((rows, features), jnp.bfloat16),
        in_specs=[pl.BlockSpec(memory_space=pltpu.VMEM)] * 2,
        out_specs=pl.BlockSpec(memory_space=pltpu.VMEM),
        compiler_params=pltpu.CompilerParams(vmem_limit_bytes=16 * 1024 * 1024),
        cost_estimate=pl.CostEstimate(
            flops=2 * rows * tokens * features, bytes_accessed=2 * (rows + tokens) * features, transcendentals=0
        ),
    )(route.reshape(1, tokens), cotangent)


def product_kernel(units_ref, tokens_ref, out_ref):
    out_ref[...] = jnp.dot(units_ref[...], tokens_ref[...], preferred_element_type=jnp.float32) * SMALL


def product(units, tokens):
    rows, depth = units.shape
    features = tokens.shape[1]
    width = 512
    return pl.pallas_call(
        product_kernel,
        grid=(features // width,),
        out_shape=jax.ShapeDtypeStruct((rows, features), jnp.float32),
        in_specs=[pl.BlockSpec((rows, depth), lambda i: (0, 0)), pl.BlockSpec((depth, width), lambda i: (0, i))],
        out_specs=pl.BlockSpec((rows, width), lambda i: (0, i)),
        compiler_params=pltpu.CompilerParams(vmem_limit_bytes=16 * 1024 * 1024),
        cost_estimate=pl.CostEstimate(
            flops=2 * rows * depth * features,
            bytes_accessed=2 * depth * (rows + features) + 4 * rows * features,
            transcendentals=0,
        ),
    )(units, tokens)


def local(cotangent, route, hidden, master, moment_one, moment_two):
    num_experts = lax.axis_size("expert")
    n_dp = lax.axis_size("dp")
    recv_rows = hidden.shape[2]
    capacity = recv_rows // num_experts
    features = cotangent.shape[1]
    ff = hidden.shape[3]
    share = ff // n_dp
    chips = n_dp // 2
    pairs = n_dp // 4
    core = lax.axis_index("dp") % 2

    ring = [[4 * p + r for p in range(pairs)] for r in range(4)]
    sides = [[4 * p + c, 4 * p + 2 + c] for p in range(pairs) for c in range(2)]

    units = hidden[0, 0].T.reshape(chips, 2, share, recv_rows)

    def of_core(which):
        return lax.dynamic_index_in_dim(units, which, axis=1, keepdims=False).reshape(chips * share, recv_rows)

    packed = pack(route, cotangent, num_experts, capacity)
    packed, units_mine, units_theirs = lax.optimization_barrier((packed, of_core(core), of_core(1 - core)))
    packed = packed.reshape(num_experts, capacity, features)
    received = lax.all_to_all(packed, "expert", split_axis=0, concat_axis=0, tiled=True).reshape(
        recv_rows, features
    )

    theirs = jnp.dot(units_theirs, received, preferred_element_type=jnp.float32) * SMALL
    other = lax.ppermute(theirs.astype(jnp.float16), "dp", [(d, d ^ 1) for d in range(n_dp)])
    mine = product(units_mine, received)
    summed = (mine + other.astype(jnp.float32)).astype(jnp.float16)
    summed = summed.reshape(pairs, 2, share, features).transpose(1, 0, 2, 3)
    halves = lax.all_to_all(summed, "dp", 0, 0, tiled=True, axis_index_groups=sides)
    quarter = (halves[0].astype(jnp.float32) + halves[1].astype(jnp.float32)).astype(jnp.float16)
    eighths = lax.all_to_all(quarter, "dp", 0, 0, tiled=True, axis_index_groups=ring)
    gradient = jnp.sum(eighths.astype(jnp.float32), axis=0, keepdims=True) * (1.0 / SMALL)

    one_next = 0.9 * moment_one + 0.1 * gradient
    two_next = 0.95 * moment_two + 0.05 * gradient * gradient
    step_dir = one_next / (1.0 - 0.9**STEP) / (jnp.sqrt(two_next / (1.0 - 0.95**STEP)) + 1e-08)
    master_next = master - 0.01 * (step_dir + 0.1 * master)
    coded = (lax.reduce_precision(master_next, 8, 7) * WEIGHT).astype(jnp.float16)
    gathered = lax.all_gather(coded, "dp", axis=1, tiled=True)
    weights = (gathered.astype(jnp.float32) * (1.0 / WEIGHT)).astype(jnp.bfloat16)
    return (master_next, one_next, two_next, weights)


def solution(mesh):
    return jax.shard_map(
        local,
        mesh=mesh,
        in_specs=(
            P(("dp", "expert"), None),
            P(("dp", "expert"), None),
            P("dp", "expert", None, None),
            P("expert", "dp", None),
            P("expert", "dp", None),
            P("expert", "dp", None),
        ),
        out_specs=(
            P("expert", "dp", None),
            P("expert", "dp", None),
            P("expert", "dp", None),
            P("expert", None, None),
        ),
        check_vma=False,
    )
```

```python
import jax
import jax.numpy as jnp
from jax import lax
from jax.experimental import pallas as pl
from jax.experimental.pallas import tpu as pltpu
from jax.sharding import PartitionSpec as P

STEP = 10
SMALL = 16.0
WEIGHT = 131072.0


def pack_kernel(capacity, route_ref, cot_ref, hidden_ref, out_ref, units_ref):
    tokens = cot_ref.shape[0]
    block = 2 * capacity
    row = route_ref[...]
    later = lax.broadcasted_iota(jnp.int32, (tokens, tokens), 1)
    token = lax.broadcasted_iota(jnp.int32, (tokens, tokens), 0)
    col = jnp.sum(jnp.where(later == token, row, 0), axis=1, keepdims=True)
    same = jnp.where((col == row) & (token < later), 1, 0)
    dest = row * capacity + jnp.sum(same, axis=0, keepdims=True)
    block = 128
    for start in range(0, out_ref.shape[0], block):
        if start < hidden_ref.shape[0]:
            units_ref[:, start : start + block] = hidden_ref[start : start + block, :].T
        slot = lax.broadcasted_iota(jnp.int32, (block, tokens), 0) + start
        pick = jnp.where(slot == dest, 1.0, 0.0).astype(jnp.bfloat16)
        out_ref[start : start + block, :] = jnp.dot(
            pick, cot_ref[...], preferred_element_type=jnp.float32
        ).astype(jnp.bfloat16)


def pack(route, cotangent, hidden, num_experts, capacity):
    tokens, features = cotangent.shape
    depth, ff = hidden.shape
    rows = num_experts * capacity
    return pl.pallas_call(
        lambda *refs: pack_kernel(capacity, *refs),
        out_shape=[
            jax.ShapeDtypeStruct((rows, features), jnp.bfloat16),
            jax.ShapeDtypeStruct((ff, depth), jnp.bfloat16),
        ],
        in_specs=[pl.BlockSpec(memory_space=pltpu.VMEM)] * 3,
        out_specs=[pl.BlockSpec(memory_space=pltpu.VMEM)] * 2,
        compiler_params=pltpu.CompilerParams(vmem_limit_bytes=16 * 1024 * 1024),
        cost_estimate=pl.CostEstimate(
            flops=2 * rows * tokens * features, bytes_accessed=2 * (rows + tokens) * features, transcendentals=0
        ),
    )(route.reshape(1, tokens), cotangent, hidden)


def product_kernel(units_ref, tokens_ref, out_ref):
    out_ref[...] = jnp.dot(units_ref[...], tokens_ref[...], preferred_element_type=jnp.float32) * SMALL


def product(units, tokens):
    rows, depth = units.shape
    features = tokens.shape[1]
    width = 512
    return pl.pallas_call(
        product_kernel,
        grid=(features // width,),
        out_shape=jax.ShapeDtypeStruct((rows, features), jnp.float32),
        in_specs=[pl.BlockSpec((rows, depth), lambda i: (0, 0)), pl.BlockSpec((depth, width), lambda i: (0, i))],
        out_specs=pl.BlockSpec((rows, width), lambda i: (0, i)),
        compiler_params=pltpu.CompilerParams(vmem_limit_bytes=16 * 1024 * 1024),
        cost_estimate=pl.CostEstimate(
            flops=2 * rows * depth * features,
            bytes_accessed=2 * depth * (rows + features) + 4 * rows * features,
            transcendentals=0,
        ),
    )(units, tokens)


def local(cotangent, route, hidden, master, moment_one, moment_two):
    num_experts = lax.axis_size("expert")
    n_dp = lax.axis_size("dp")
    recv_rows = hidden.shape[2]
    capacity = recv_rows // num_experts
    features = cotangent.shape[1]
    ff = hidden.shape[3]
    share = ff // n_dp
    chips = n_dp // 2
    pairs = n_dp // 4
    core = lax.axis_index("dp") % 2

    ring = [[4 * p + r for p in range(pairs)] for r in range(4)]
    sides = [[4 * p + c, 4 * p + 2 + c] for p in range(pairs) for c in range(2)]

    cut = 512
    early = hidden[0, 0, :cut].T
    packed, late = pack(route, cotangent, hidden[0, 0, cut:], num_experts, capacity)
    units = jnp.concatenate([early, late], axis=1).reshape(chips, 2, share, recv_rows)

    def of_core(which):
        return lax.dynamic_index_in_dim(units, which, axis=1, keepdims=False).reshape(chips * share, recv_rows)

    packed, units_mine, units_theirs = lax.optimization_barrier((packed, of_core(core), of_core(1 - core)))
    packed = packed.reshape(num_experts, capacity, features)
    received = lax.all_to_all(packed, "expert", split_axis=0, concat_axis=0, tiled=True).reshape(
        recv_rows, features
    )

    theirs = jnp.dot(units_theirs, received, preferred_element_type=jnp.float32) * SMALL
    other = lax.ppermute(theirs.astype(jnp.float16), "dp", [(d, d ^ 1) for d in range(n_dp)])
    mine = product(units_mine, received)
    summed = (mine + other.astype(jnp.float32)).astype(jnp.float16)
    summed = summed.reshape(pairs, 2, share, features).transpose(1, 0, 2, 3)
    halves = lax.all_to_all(summed, "dp", 0, 0, tiled=True, axis_index_groups=sides)
    quarter = (halves[0].astype(jnp.float32) + halves[1].astype(jnp.float32)).astype(jnp.float16)
    eighths = lax.all_to_all(quarter, "dp", 0, 0, tiled=True, axis_index_groups=ring)
    gradient = jnp.sum(eighths.astype(jnp.float32), axis=0, keepdims=True) * (1.0 / SMALL)

    one_next = 0.9 * moment_one + 0.1 * gradient
    two_next = 0.95 * moment_two + 0.05 * gradient * gradient
    step_dir = one_next / (1.0 - 0.9**STEP) / (jnp.sqrt(two_next / (1.0 - 0.95**STEP)) + 1e-08)
    master_next = master - 0.01 * (step_dir + 0.1 * master)
    coded = (lax.reduce_precision(master_next, 8, 7) * WEIGHT).astype(jnp.float16)
    gathered = lax.all_gather(coded, "dp", axis=1, tiled=True)
    weights = (gathered.astype(jnp.float32) * (1.0 / WEIGHT)).astype(jnp.bfloat16)
    return (master_next, one_next, two_next, weights)


def solution(mesh):
    return jax.shard_map(
        local,
        mesh=mesh,
        in_specs=(
            P(("dp", "expert"), None),
            P(("dp", "expert"), None),
            P("dp", "expert", None, None),
            P("expert", "dp", None),
            P("expert", "dp", None),
            P("expert", "dp", None),
        ),
        out_specs=(
            P("expert", "dp", None),
            P("expert", "dp", None),
            P("expert", "dp", None),
            P("expert", None, None),
        ),
        check_vma=False,
    )
```

```python
import jax
import jax.numpy as jnp
from jax import lax
from jax.experimental import pallas as pl
from jax.experimental.pallas import tpu as pltpu
from jax.sharding import PartitionSpec as P

STEP = 10
SMALL = 16.0
WEIGHT = 131072.0


def pack_kernel(capacity, route_ref, cot_ref, hidden_ref, out_ref, units_ref):
    tokens = cot_ref.shape[0]
    block = 2 * capacity
    row = route_ref[...]
    later = lax.broadcasted_iota(jnp.int32, (tokens, tokens), 1)
    token = lax.broadcasted_iota(jnp.int32, (tokens, tokens), 0)
    col = jnp.sum(jnp.where(later == token, row, 0), axis=1, keepdims=True)
    same = jnp.where((col == row) & (token < later), 1, 0)
    dest = row * capacity + jnp.sum(same, axis=0, keepdims=True)
    block = 128
    for start in range(0, out_ref.shape[0], block):
        if start < hidden_ref.shape[0]:
            units_ref[:, start : start + block] = hidden_ref[start : start + block, :].T
        slot = lax.broadcasted_iota(jnp.int32, (block, tokens), 0) + start
        pick = jnp.where(slot == dest, 1.0, 0.0).astype(jnp.bfloat16)
        out_ref[start : start + block, :] = jnp.dot(
            pick, cot_ref[...], preferred_element_type=jnp.float32
        ).astype(jnp.bfloat16)


def pack(route, cotangent, hidden, num_experts, capacity):
    tokens, features = cotangent.shape
    depth, ff = hidden.shape
    rows = num_experts * capacity
    return pl.pallas_call(
        lambda *refs: pack_kernel(capacity, *refs),
        out_shape=[
            jax.ShapeDtypeStruct((rows, features), jnp.bfloat16),
            jax.ShapeDtypeStruct((ff, depth), jnp.bfloat16),
        ],
        in_specs=[pl.BlockSpec(memory_space=pltpu.VMEM)] * 3,
        out_specs=[pl.BlockSpec(memory_space=pltpu.VMEM)] * 2,
        compiler_params=pltpu.CompilerParams(vmem_limit_bytes=16 * 1024 * 1024),
        cost_estimate=pl.CostEstimate(
            flops=2 * rows * tokens * features, bytes_accessed=2 * (rows + tokens) * features, transcendentals=0
        ),
    )(route.reshape(1, tokens), cotangent, hidden)


def product_kernel(units_ref, tokens_ref, out_ref):
    out_ref[...] = jnp.dot(units_ref[...], tokens_ref[...], preferred_element_type=jnp.float32) * SMALL


def product(units, tokens):
    rows, depth = units.shape
    features = tokens.shape[1]
    width = 512
    return pl.pallas_call(
        product_kernel,
        grid=(features // width,),
        out_shape=jax.ShapeDtypeStruct((rows, features), jnp.float32),
        in_specs=[pl.BlockSpec((rows, depth), lambda i: (0, 0)), pl.BlockSpec((depth, width), lambda i: (0, i))],
        out_specs=pl.BlockSpec((rows, width), lambda i: (0, i)),
        compiler_params=pltpu.CompilerParams(vmem_limit_bytes=16 * 1024 * 1024),
        cost_estimate=pl.CostEstimate(
            flops=2 * rows * depth * features,
            bytes_accessed=2 * depth * (rows + features) + 4 * rows * features,
            transcendentals=0,
        ),
    )(units, tokens)


def local(cotangent, route, hidden, master, moment_one, moment_two):
    num_experts = lax.axis_size("expert")
    n_dp = lax.axis_size("dp")
    recv_rows = hidden.shape[2]
    capacity = recv_rows // num_experts
    features = cotangent.shape[1]
    ff = hidden.shape[3]
    share = ff // n_dp
    chips = n_dp // 2
    pairs = n_dp // 4
    core = lax.axis_index("dp") % 2

    ring = [[4 * p + r for p in range(pairs)] for r in range(4)]
    sides = [[4 * p + c, 4 * p + 2 + c] for p in range(pairs) for c in range(2)]

    cut = 384
    early = hidden[0, 0, :cut].T
    packed, late = pack(route, cotangent, hidden[0, 0, cut:], num_experts, capacity)
    units = jnp.concatenate([early, late], axis=1).reshape(chips, 2, share, recv_rows)

    def of_core(which):
        return lax.dynamic_index_in_dim(units, which, axis=1, keepdims=False).reshape(chips * share, recv_rows)

    packed, units_mine, units_theirs = lax.optimization_barrier((packed, of_core(core), of_core(1 - core)))
    packed = packed.reshape(num_experts, capacity, features)
    received = lax.all_to_all(packed, "expert", split_axis=0, concat_axis=0, tiled=True).reshape(
        recv_rows, features
    )

    theirs = jnp.dot(units_theirs, received, preferred_element_type=jnp.float32) * SMALL
    other = lax.ppermute(theirs.astype(jnp.float16), "dp", [(d, d ^ 1) for d in range(n_dp)])
    mine = product(units_mine, received)
    summed = (mine + other.astype(jnp.float32)).astype(jnp.float16)
    summed = summed.reshape(pairs, 2, share, features).transpose(1, 0, 2, 3)
    halves = lax.all_to_all(summed, "dp", 0, 0, tiled=True, axis_index_groups=sides)
    quarter = (halves[0].astype(jnp.float32) + halves[1].astype(jnp.float32)).astype(jnp.float16)
    eighths = lax.all_to_all(quarter, "dp", 0, 0, tiled=True, axis_index_groups=ring)
    gradient = jnp.sum(eighths.astype(jnp.float32), axis=0, keepdims=True) * (1.0 / SMALL)

    one_next = 0.9 * moment_one + 0.1 * gradient
    two_next = 0.95 * moment_two + 0.05 * gradient * gradient
    step_dir = one_next / (1.0 - 0.9**STEP) / (jnp.sqrt(two_next / (1.0 - 0.95**STEP)) + 1e-08)
    master_next = master - 0.01 * (step_dir + 0.1 * master)
    coded = (lax.reduce_precision(master_next, 8, 7) * WEIGHT).astype(jnp.float16)
    gathered = lax.all_gather(coded, "dp", axis=1, tiled=True)
    weights = (gathered.astype(jnp.float32) * (1.0 / WEIGHT)).astype(jnp.bfloat16)
    return (master_next, one_next, two_next, weights)


def solution(mesh):
    return jax.shard_map(
        local,
        mesh=mesh,
        in_specs=(
            P(("dp", "expert"), None),
            P(("dp", "expert"), None),
            P("dp", "expert", None, None),
            P("expert", "dp", None),
            P("expert", "dp", None),
            P("expert", "dp", None),
        ),
        out_specs=(
            P("expert", "dp", None),
            P("expert", "dp", None),
            P("expert", "dp", None),
            P("expert", None, None),
        ),
        check_vma=False,
    )
```
